32 devices in a mesh: px: 4 (over z), py: 2 (over x), dz: 4 (over y, core).
Axes of the slice: x: 2, y: 2, z: 4, core: 2. Of those that a mesh axis runs over, the one named last changes fastest.
Arguments:
- near_state: float32 [3, 32, 192, 512], P(None, 'px', 'dz', 'py'), may hold values from -1 to 1, as said below
- column_owner: int32 [4, 8, 512, 1], P('px', ('py', 'dz')), may hold values from 0 to 7; in each aligned block of 512 rows (0 to 511, 512 to 1023, ..., all dimensions but the last counted through in order) at most 128 rows name the same one
- landing: int32 [4, 8, 512], P('px', ('py', 'dz')), may hold values from 0 to 16383
- far_depth: float32 [256, 2048], P('px', ('py', 'dz')), may hold values from 3 to 6
- far_flows: float32 [2, 256, 2048], P(None, 'px', ('py', 'dz')), may hold values from -3 to 3
- wet_mask: int32 [256, 2048], P('px', ('py', 'dz')), may hold values 0 or 1
Outputs:
- near_fraction: float32 [32, 192, 512], P('px', 'dz', 'py')
- far_new: float32 [3, 256, 2048], P(None, 'px', ('py', 'dz'))
The draws below stay inside these ranges and needn't reach their ends.
Inputs may be any that keep to these rules, and one draw needn't show every extreme that they name: `near_state`: the volume fraction (first field) lies in 0 to 1; the velocities lie in -1 to 1. `column_owner`: in each near tile no owner receives more than 128 columns; some owner receives exactly 128.
All inputs are finite; a program needn't handle non-finite values. No bound on the sum of `wet_mask` on one device may be relied on, other than what follows from the above.
Results may differ from the reference program's by a relative error of at most 0.00002.
Values sent between devices are 32-bit elements; how exact they have to be, the bound alone decides.
A program may use at most 64 MiB of HBM per device.

```python
import math
import jax
import jax.numpy as jnp
import numpy as np
from jax import lax

CX = 8
FX = 64
FY = 256
CAP = 128
NXN = 32
NYN = 512
NZN = 192
NDEST = 8
QY = 64
NCOL = 512
FNX = 256
FNY = 2048
N_PX = 4


def draw_near_state(key, part):
    subkeys = jax.random.split(key, 4)
    cell_shape = (NXN, NZN, NYN)
    column_shape = (NXN, 1, NYN)
    column_factor = jax.random.uniform(subkeys[0], column_shape, jnp.float32, 0.3, 1.0)
    cell_factor = jax.random.uniform(subkeys[1], cell_shape, jnp.float32, 0.4, 1.0)
    slowest = 0.2
    fraction = column_factor * cell_factor
    speed_x = jax.random.uniform(subkeys[2], cell_shape, jnp.float32, slowest, 1.0)
    speed_y = jax.random.uniform(subkeys[3], cell_shape, jnp.float32, slowest, 1.0)
    return jnp.stack([fraction, speed_x, speed_y]).astype(jnp.float32)


def plant(drawn, own_key, least, largest):
    index_at = [jax.random.randint(jax.random.fold_in(own_key, axis), (), 0, length) for axis, length in enumerate(drawn.shape)]
    widest = drawn.shape.index(max(drawn.shape))
    neighbour = index_at[:widest] + [(index_at[widest] + 1) % drawn.shape[widest]] + index_at[widest + 1:]
    return drawn.at[tuple(index_at)].set(least).at[tuple(neighbour)].set(largest)


def steps_of(own_key, extent, shards, low, high):
    level, own = 1.0, jax.random.fold_in(own_key, 6)
    for dim, parts in shards:
        heights = jnp.exp(jax.random.uniform(jax.random.fold_in(own, dim), (parts,), jnp.float32, low / len(shards), high / len(shards)))
        level = level * jnp.repeat(heights, extent[dim] // parts).reshape([-1 if axis == dim else 1 for axis in range(len(extent))])
    return level


def routed_block(rng, own, number, rows, number_of, top, most, skew):
    sequence = jax.random.permutation(rng, number_of)
    heavy_load, common = portions_of(number_of, rows * top, most, skew, True), portions_of(number_of, rows * top, most, skew, False)
    places = jnp.arange(number_of)

    def named(sizes, offset_by):
        used = int((sizes > 0).sum())
        fixed = max(1, used // 4)
        moved = fixed + (places - fixed + offset_by * (used - fixed)) % max(1, number_of - fixed)
        return jnp.zeros((number_of,), jnp.int32).at[sequence[jnp.where(places < fixed, places, moved)]].set(jnp.asarray(sizes, jnp.int32))

    sizes = jnp.where(number % 4 == 0, named(heavy_load, number // 4), named(common, number - number // 4 - 1))
    mixed = jax.random.permutation(jax.random.fold_in(own, 3), number_of)
    source_of, sink = mixed[0:number_of // 2 * 2:2], mixed[1:number_of // 2 * 2:2]
    margin = jnp.minimum(sizes[source_of] - 1, most - sizes[sink]) // 2
    margin = jnp.where((source_of == sequence[0]) | (sink == sequence[0]) | (sizes[sink] == 0), 0, jnp.maximum(margin, 0))
    moved = jax.random.randint(jax.random.fold_in(own, 4), (number_of // 2,), 0, 1 << 20) % (margin + 1)
    sizes = sizes.at[source_of].add(-moved).at[sink].add(moved)
    members = jnp.searchsorted(jnp.cumsum(sizes), jnp.arange(rows * top), side="right").astype(jnp.int32)
    grid = members.reshape(top, rows).T
    grid = grid[jax.random.permutation(jax.random.fold_in(own, 1), rows)]
    offset_by = jax.random.randint(jax.random.fold_in(own, 2), (rows, 1), 0, top)
    return jnp.take_along_axis(grid, (jnp.arange(top)[None, :] + offset_by) % top, axis=1)


def portions_of(count, total, most, lean, full):
    portions = [(1 << 20) // math.isqrt(standing ** lean) + 1 for standing in range(1, count + 1)]
    largest = most if full else min(most, max(-(-total // count), total * portions[0] // sum(portions)))
    least = 1 if total - largest >= count - 1 else 0
    counts, surplus = [largest] + [least] * (count - 1), total - largest - least * (count - 1)
    while surplus > 0:
        candidates = [i for i in range(1, count) if counts[i] < largest] or [i for i in range(1, count) if counts[i] < most]
        pool, budget = sum([portions[i] for i in candidates]), surplus
        for i in candidates:
            extra = min(most - counts[i], max(1, budget * portions[i] // pool), surplus)
            counts[i] = counts[i] + extra
            surplus = surplus - extra
    return np.array(counts)


def centred(stream_key, extent, spread, most, pieces=(), held_as=jnp.bfloat16):
    drawn = spread * jax.random.normal(stream_key, extent, jnp.float32)
    if pieces:
        drawn = drawn * steps_of(stream_key, extent, pieces, -0.22, 0.18)
    return jnp.clip(drawn, -most, most).astype(held_as)


def setup_inputs(seed: int = 0) -> dict:
    streams_of = jax.random.split(jax.random.key(seed), 7)
    near_state = draw_near_state(jax.random.fold_in(streams_of[6], 71), 0)
    column_owner_keys = jax.random.split(jax.random.fold_in(streams_of[1], 1), N_PX * NDEST * NCOL // NCOL)
    column_owner_turns = jax.random.permutation(jax.random.fold_in(streams_of[1], 3), N_PX * NDEST * NCOL // NCOL)
    column_owner = jax.vmap(lambda own, number: routed_block(jax.random.fold_in(streams_of[1], 2), own, number, NCOL, NDEST, 1, CAP, 2))(column_owner_keys, column_owner_turns).reshape((N_PX, NDEST, NCOL, 1))
    landing = plant(jax.random.randint(streams_of[2], (N_PX, NDEST, NCOL), 0, FX * FY), jax.random.fold_in(streams_of[2], 1), 0, (FX * FY) - 1).astype(jnp.int32)
    far_depth = jnp.clip(3.0 + 3.0 * jax.random.uniform(streams_of[3], (FNX, FNY), jnp.float32) ** steps_of(streams_of[3], (FNX, FNY), ((0, 4), (1, 8)), -0.2, 0.2), 3.0, 6.0)
    far_flows = centred(streams_of[4], (2, FNX, FNY), 0.5, 3.0, ((1, 4), (2, 8)), jnp.float32)
    wet_mask = plant((jax.random.randint(streams_of[5], (FNX, FNY), 0, 5) < 4).astype(jnp.int32), jax.random.fold_in(streams_of[5], 1), 0, 1)
    return dict(near_state=near_state, column_owner=column_owner, landing=landing, far_depth=far_depth, far_flows=far_flows, wet_mask=wet_mask)


advect_coef = 0.25
diffuse_coef = 0.1
slope_coef = 0.5
flux_coef = 0.1
gravity = 1.0
column_height = 4.0


def near_update(center, xplus, xminus, yplus, yminus, zplus, zminus):
    velx = center[1]
    vely = center[2]
    lap = xplus + xminus + yplus + yminus + zplus + zminus - 6.0 * center
    moved = center - advect_coef * (velx * (xplus - xminus) + vely * (yplus - yminus)) + diffuse_coef * lap
    new_frac = moved[0]
    new_velx = moved[1] - slope_coef * (xplus[0] - xminus[0])
    new_vely = moved[2] - slope_coef * (yplus[0] - yminus[0])
    return new_frac, new_velx, new_vely


def far_update(padded):
    state = padded[0:3]
    xflux = padded[3:6]
    yflux = padded[6:9]
    avg = 0.25 * (state[:, 2:, 1:-1] + state[:, :-2, 1:-1] + state[:, 1:-1, 2:] + state[:, 1:-1, :-2])
    return avg - flux_coef * (xflux[:, 2:, 1:-1] - xflux[:, :-2, 1:-1]) - flux_coef * (yflux[:, 1:-1, 2:] - yflux[:, 1:-1, :-2])


def fluxes(state):
    depth = state[0]
    flow_x = state[1]
    flow_y = state[2]
    cross = flow_x * flow_y / depth
    press = 0.5 * gravity * depth * depth
    xflux = jnp.stack([flow_x, flow_x * flow_x / depth + press, cross])
    yflux = jnp.stack([flow_y, cross, flow_y * flow_y / depth + press])
    return xflux, yflux


def reference(near_state, column_owner, landing, far_depth, far_flows, wet_mask):
    padded = jnp.pad(near_state, ((0, 0), (1, 1), (1, 1), (1, 1)))
    inv_depth = column_height / NZN

    def tile(index):
        sl = lax.dynamic_slice_in_dim(padded, index * CX, CX + 2, 1)
        center = sl[:, 1:-1, 1:-1, 1:-1]
        new_frac, new_velx, new_vely = near_update(center, sl[:, 2:, 1:-1, 1:-1], sl[:, :-2, 1:-1, 1:-1], sl[:, 1:-1, 1:-1, 2:], sl[:, 1:-1, 1:-1, :-2], sl[:, 1:-1, 2:, 1:-1], sl[:, 1:-1, :-2, 1:-1])
        sums = jnp.stack([jnp.sum(new_frac, axis=1), jnp.sum(new_frac * new_velx, axis=1), jnp.sum(new_frac * new_vely, axis=1)]) * inv_depth
        return new_frac, sums

    fracs, sums = lax.map(tile, jnp.arange(N_PX, dtype=jnp.int32))
    near_fraction = fracs.reshape(NXN, NZN, NYN)
    columns = jnp.transpose(sums, (1, 0, 2, 3)).reshape(3, N_PX, CX, NDEST, QY)
    columns = jnp.transpose(columns, (0, 1, 3, 2, 4)).reshape(3, N_PX * NDEST * NCOL)
    owner = column_owner[..., 0]
    tile_x = jnp.arange(N_PX, dtype=jnp.int32)[:, None, None]
    glob_x = tile_x * FX + landing // FY
    glob_y = owner * FY + landing % FY
    flat = (glob_x * FNY + glob_y).reshape(-1)
    source = jnp.zeros((3, FNX * FNY), jnp.float32).at[:, flat].add(columns).reshape(3, FNX, FNY)
    wet = wet_mask.astype(jnp.float32)
    state = jnp.stack([far_depth, far_flows[0], far_flows[1]]) + source
    state = jnp.stack([state[0], state[1] * wet, state[2] * wet])
    xflux, yflux = fluxes(state)
    stacked = jnp.concatenate([state, xflux, yflux], axis=0)
    far_new = far_update(jnp.pad(stacked, ((0, 0), (1, 1), (1, 1))))
    return near_fraction, far_new
```

```python
import functools

import jax
import jax.numpy as jnp
from jax import lax
from jax.experimental import pallas as pl
from jax.experimental.pallas import tpu as pltpu
from jax.sharding import PartitionSpec as P

advect_coef = 0.25
diffuse_coef = 0.1
slope_coef = 0.5
flux_coef = 0.1
gravity = 1.0
column_height = 4.0

LANES = 128
PARTS = 3


def kernel(sizes, near, ids, far_in, wet_in, frac_out, far_out,
           x, nf, yedge, yhalo, zedge, zhalo, idall, sums, a_mat, b_mat, q, wet, fdep, fedge_r, fhalo_r, fedge_c, fhalo_c,
           fout, loc_sem, hs, hr, ids_s, ids_r, sum_s, sum_r):
    n_px, n_py, n_dz = sizes
    group = n_py * n_dz
    nx, nz, ny = near.shape[1:]
    fx, fy = wet_in.shape
    px, py, dz = lax.axis_index("px"), lax.axis_index("py"), lax.axis_index("dz")
    me = py * n_dz + dz

    def member(d):
        return {"px": px, "py": d // n_dz, "dz": d % n_dz}

    def peer(o):
        return lax.rem(me + o, group)

    def source(o):
        return lax.rem(me + group - o, group)

    up, down = {"px": px + 1, "py": py, "dz": dz}, {"px": px - 1, "py": py, "dz": dz}
    has_up, has_down = px < n_px - 1, px > 0

    barrier = pltpu.get_barrier_semaphore()
    for o in range(1, group):
        pl.semaphore_signal(barrier, inc=1, device_id=member(peer(o)))

    @pl.when(has_up)
    def _():
        pl.semaphore_signal(barrier, inc=1, device_id=up)

    @pl.when(has_down)
    def _():
        pl.semaphore_signal(barrier, inc=1, device_id=down)

    load_x = pltpu.make_async_copy(near, x.at[:, pl.ds(1, nx), pl.ds(8, nz), :], loc_sem.at[0])
    load_far = pltpu.make_async_copy(far_in, fdep, loc_sem.at[1])
    load_wet = pltpu.make_async_copy(wet_in, wet, loc_sem.at[2])
    load_ids = pltpu.make_async_copy(ids, idall.at[me], loc_sem.at[3])
    load_x.start()
    load_far.start()
    load_wet.start()
    load_ids.start()

    pl.semaphore_wait(barrier, group - 1 + has_up.astype(jnp.int32) + has_down.astype(jnp.int32))

    def send(src, dst, i, where):
        return pltpu.make_async_remote_copy(src_ref=src, dst_ref=dst, send_sem=hs.at[i], recv_sem=hr.at[i], device_id=where)

    rows = pl.ds(8, nz)
    x_up = send(near.at[:, nx - 1], x.at[:, 0, rows, :], 0, up)
    x_down = send(near.at[:, 0], x.at[:, nx + 1, rows, :], 1, down)
    y_up = send(yedge.at[0], yhalo.at[0], 2, {"px": px, "py": py + 1, "dz": dz})
    y_down = send(yedge.at[1], yhalo.at[1], 3, {"px": px, "py": py - 1, "dz": dz})
    z_up = send(zedge.at[0], zhalo.at[0], 4, {"px": px, "py": py, "dz": dz + 1})
    z_down = send(zedge.at[1], zhalo.at[1], 5, {"px": px, "py": py, "dz": dz - 1})
    fr_up = send(fedge_r.at[0], fhalo_r.at[0], 6, up)
    fr_down = send(fedge_r.at[1], fhalo_r.at[1], 7, down)
    fc_up = send(fedge_c.at[0], fhalo_c.at[0], 8, member(me + 1))
    fc_down = send(fedge_c.at[1], fhalo_c.at[1], 9, member(me - 1))
    near_y = ((y_up, py < n_py - 1, py > 0, yhalo.at[0]), (y_down, py > 0, py < n_py - 1, yhalo.at[1]))
    near_z = ((z_up, dz < n_dz - 1, dz > 0, zhalo.at[0]), (z_down, dz > 0, dz < n_dz - 1, zhalo.at[1]))
    near_x = ((x_up, has_up, has_down, x.at[:, 0]), (x_down, has_down, has_up, x.at[:, nx + 1]))
    far_r = ((fr_up, has_up, has_down, fhalo_r.at[0]), (fr_down, has_down, has_up, fhalo_r.at[1]))
    far_c = ((fc_up, me < group - 1, me > 0, fhalo_c.at[0]), (fc_down, me > 0, me < group - 1, fhalo_c.at[1]))

    def start(pairs):
        for copy, out, _, _ in pairs:
            pl.when(out)(copy.start)

    def clear(pairs):
        for _, _, into, halo in pairs:
            @pl.when(jnp.logical_not(into))
            def _():
                halo[...] = jnp.zeros(halo.shape, jnp.float32)

    def arrive(pairs):
        for copy, _, into, _ in pairs:
            pl.when(into)(copy.wait_recv)

    def sent(pairs):
        for copy, out, _, _ in pairs:
            pl.when(out)(copy.wait_send)

    start(near_x)
    for pairs in (near_x, near_y, near_z, far_r, far_c):
        clear(pairs)

    load_x.wait()
    lane = lax.broadcasted_iota(jnp.int32, (nz, LANES), 1)
    for f in range(3):
        for i in range(nx):
            zedge[0, f, pl.ds(i, 1), :] = x[f, i + 1, pl.ds(nz + 7, 1), :]
            zedge[1, f, pl.ds(i, 1), :] = x[f, i + 1, pl.ds(8, 1), :]
    start(near_z)
    high = jnp.zeros((nz, LANES), jnp.float32)
    low = jnp.zeros((nz, LANES), jnp.float32)
    for i in range(nx):
        for f in range(3):
            k = 3 * i + f
            high = jnp.where(lane == k, pltpu.roll(x[f, i + 1, rows, ny - LANES:], (k + 1) % LANES, 1), high)
            first = x[f, i + 1, rows, :LANES]
            low = jnp.where(lane == k, pltpu.roll(first, k, 1) if k else first, low)
    yedge[0] = high
    yedge[1] = low
    start(near_y)

    load_ids.wait()

    def id_copy(o, d):
        return pltpu.make_async_remote_copy(
            src_ref=idall.at[me], dst_ref=idall.at[d], send_sem=ids_s.at[o], recv_sem=ids_r.at[o], device_id=member(peer(o)))

    for o in range(1, group):
        id_copy(o, me).start()

    arrive(near_z)
    for f in range(3):
        for i in range(nx):
            x[f, i + 1, pl.ds(7, 1), :] = zhalo[0, f, pl.ds(i, 1), :]
            x[f, i + 1, pl.ds(nz + 8, 1), :] = zhalo[1, f, pl.ds(i, 1), :]
    arrive(near_y)

    col = lax.broadcasted_iota(jnp.int32, (8, ny), 1)

    def plane(i):
        total = [jnp.zeros((8, ny), jnp.float32) for _ in range(3)]
        shift = (LANES - 3 * i) % LANES if isinstance(i, int) else lax.rem(LANES - 3 * i, LANES)
        for c in range(0, nz, 8):
            here = pl.ds(8 + c, 8)
            ylo = pltpu.roll(yhalo[0, pl.ds(c, 8), :], shift, 1)
            yhi = pltpu.roll(yhalo[1, pl.ds(c, 8), :], shift, 1)
            u, v = x[1, i + 1, here, :], x[2, i + 1, here, :]
            moved, slopes = [], None
            for f in range(3):
                mid = x[f, i + 1, here, :]
                xp, xm = x[f, i + 2, here, :], x[f, i, here, :]
                zp, zm = x[f, i + 1, pl.ds(9 + c, 8), :], x[f, i + 1, pl.ds(7 + c, 8), :]
                yp = jnp.where(col == ny - 1, yhi[:, f:f + 1], pltpu.roll(mid, ny - 1, 1))
                ym = jnp.where(col == 0, ylo[:, f:f + 1], pltpu.roll(mid, 1, 1))
                dx, dy = xp - xm, yp - ym
                lap = xp + xm + yp + ym + zp + zm - 6.0 * mid
                moved.append(mid - advect_coef * (u * dx + v * dy) + diffuse_coef * lap)
                if f == 0:
                    slopes = (dx, dy)
            nf[i, pl.ds(c, 8), :] = moved[0]
            total[0] += moved[0]
            total[1] += moved[0] * (moved[1] - slope_coef * slopes[0])
            total[2] += moved[0] * (moved[2] - slope_coef * slopes[1])
        for f in range(3):
            sums[me, f, pl.ds(i, 1), :] = jnp.sum(total[f], axis=0, keepdims=True)

    def inner(i, carry):
        plane(i)
        return carry

    lax.fori_loop(1, nx - 1, inner, 0)

    for o in range(1, group):
        id_copy(o, source(o)).wait_recv()
    row_at = []
    line = lax.broadcasted_iota(jnp.int32, (fy, ny), 0)
    for p in range(n_py):
        owner, land = idall[p * n_dz, 0], idall[p * n_dz, 1]
        for e in range(1, n_dz):
            owner = owner + idall[p * n_dz + e, 0]
            land = land + idall[p * n_dz + e, 1]
        row = lax.div(land, jnp.full_like(land, fy)) if fy & (fy - 1) else lax.shift_right_logical(land, jnp.full_like(land, fy.bit_length() - 1))
        at = land - row * fy
        row_at.append(jnp.where(owner == me, row, -1))
        for i in range(nx):
            b = (p * nx + i) * ny
            b_mat[:, pl.ds(b, ny)] = jnp.where(line == at[i:i + 1, :], 1.0, 0.0).astype(jnp.bfloat16)

    arrive(near_x)
    plane(0)
    plane(nx - 1)

    def sum_copy(o, d):
        return pltpu.make_async_remote_copy(
            src_ref=sums.at[me], dst_ref=sums.at[d], send_sem=sum_s.at[o], recv_sem=sum_r.at[o], device_id=member(peer(o)))

    for o in range(1, group):
        sum_copy(o, me).start()
    save_frac = pltpu.make_async_copy(nf, frac_out, loc_sem.at[4])
    save_frac.start()
    load_far.wait()
    load_wet.wait()
    for o in range(1, group):
        sum_copy(o, source(o)).wait_recv()

    per_column = column_height / (nz * n_dz)
    cell_row = lax.broadcasted_iota(jnp.int32, (fx, ny), 0)
    for p in range(n_py):
        parts = []
        for f in range(3):
            rest = sums[p * n_dz, f]
            for e in range(1, n_dz):
                rest = rest + sums[p * n_dz + e, f]
            rest = rest * per_column
            for s in range(PARTS):
                part = rest.astype(jnp.bfloat16).astype(jnp.float32)
                rest = rest - part
                parts.append(part)
        for i in range(nx):
            b = (p * nx + i) * ny
            hit = cell_row == row_at[p][i:i + 1, :]
            for k, part in enumerate(parts):
                a_mat[pl.ds(k * fx, fx), pl.ds(b, ny)] = jnp.where(hit, part[i:i + 1, :], 0.0).astype(jnp.bfloat16)
    landed = lax.dot_general(a_mat[...], b_mat[...], (((1,), (1,)), ((), ())), preferred_element_type=jnp.float32)
    dry = wet[...].astype(jnp.float32)
    for f in range(3):
        state = fdep[f]
        for s in range(PARTS):
            k = f * PARTS + s
            state = state + landed[k * fx:(k + 1) * fx, :]
        if f:
            state = state * dry
        q[f, pl.ds(8, fx), :] = state
        fedge_r[0, pl.ds(f, 1), :] = state[fx - 1:fx, :]
        fedge_r[1, pl.ds(f, 1), :] = state[0:1, :]
    start(far_r)
    lane = lax.broadcasted_iota(jnp.int32, (fx, LANES), 1)
    high = jnp.zeros((fx, LANES), jnp.float32)
    low = jnp.zeros((fx, LANES), jnp.float32)
    for f in range(3):
        high = jnp.where(lane == f, pltpu.roll(q[f, pl.ds(8, fx), fy - LANES:], f + 1, 1), high)
        first = q[f, pl.ds(8, fx), :LANES]
        low = jnp.where(lane == f, pltpu.roll(first, f, 1) if f else first, low)
    fedge_c[0] = high
    fedge_c[1] = low
    start(far_c)

    def fluxes(h, hu, hv, divisor):
        inverse = 1.0 / divisor
        press = 0.5 * gravity * h * h
        return hu * hu * inverse + press, hu * hv * inverse, hv * hv * inverse + press

    for c in range(8, fx + 8, 8):
        here = pl.ds(c, 8)
        h, hu, hv = q[0, here, :], q[1, here, :], q[2, here, :]
        for k, flux in enumerate(fluxes(h, hu, hv, h)):
            q[3 + k, here, :] = flux

    arrive(far_r)
    for side, there, at in ((0, has_down, 7), (1, has_up, fx + 8)):
        h, hu, hv = (fhalo_r[side, pl.ds(f, 1), :] for f in range(3))
        for k, value in enumerate((h, hu, hv) + fluxes(h, hu, hv, jnp.where(there, h, 1.0))):
            q[k, pl.ds(at, 1), :] = value
    arrive(far_c)
    col = lax.broadcasted_iota(jnp.int32, (8, fy), 1)
    for c in range(0, fx, 8):
        here = pl.ds(8 + c, 8)
        outer = []
        for side, there in ((0, me > 0), (1, me < group - 1)):
            block = fhalo_c[side, pl.ds(c, 8), :]
            h, hu, hv = block, pltpu.roll(block, LANES - 1, 1), pltpu.roll(block, LANES - 2, 1)
            outer.append([z[:, 0:1] for z in (h, hu, hv) + fluxes(h, hu, hv, jnp.where(there, h, 1.0))])

        def beside(k):
            mid = q[k, here, :]
            return (jnp.where(col == fy - 1, outer[1][k], pltpu.roll(mid, fy - 1, 1)),
                    jnp.where(col == 0, outer[0][k], pltpu.roll(mid, 1, 1)))

        above = [q[k, pl.ds(9 + c, 8), :] for k in range(5)]
        below = [q[k, pl.ds(7 + c, 8), :] for k in range(5)]
        pairs = [beside(0), beside(1), beside(2), None, beside(4), beside(5)]
        for f, (xk, yk) in enumerate(((1, 2), (3, 4), (4, 5))):
            mean = 0.25 * (above[f] + below[f] + pairs[f][0] + pairs[f][1])
            fout[f, pl.ds(c, 8), :] = (
                mean - flux_coef * (above[xk] - below[xk]) - flux_coef * (pairs[yk][0] - pairs[yk][1]))
    save_far = pltpu.make_async_copy(fout, far_out, loc_sem.at[5])
    save_far.start()

    for pairs in (near_x, near_y, near_z, far_r, far_c):
        sent(pairs)
    for o in range(1, group):
        id_copy(o, me).wait_send()
        sum_copy(o, me).wait_send()
    save_frac.wait()
    save_far.wait()


def solution(mesh):
    sizes = tuple(mesh.shape[axis] for axis in ("px", "py", "dz"))
    n_px, n_py, n_dz = sizes
    group = n_py * n_dz

    def local(near_state, column_owner, landing, far_depth, far_flows, wet_mask):
        _, nx, nz, ny = near_state.shape
        fx, fy = far_depth.shape
        qy = ny // n_dz
        ids = jnp.stack([column_owner.reshape(nx, qy), landing.reshape(nx, qy)])
        ids = lax.dynamic_update_slice(
            jnp.zeros((2, nx, ny), jnp.int32), ids, (0, 0, lax.axis_index("dz") * qy))
        far = jnp.concatenate([far_depth[None], far_flows])
        anywhere = pl.BlockSpec(memory_space=pl.ANY)
        f32 = jnp.float32
        columns = n_py * nx * ny
        return pl.pallas_call(
            functools.partial(kernel, sizes),
            out_shape=(jax.ShapeDtypeStruct((nx, nz, ny), f32), jax.ShapeDtypeStruct((3, fx, fy), f32)),
            in_specs=[anywhere] * 4,
            out_specs=(anywhere, anywhere),
            scratch_shapes=[
                pltpu.VMEM((3, nx + 2, nz + 16, ny), f32),
                pltpu.VMEM((nx, nz, ny), f32),
                pltpu.VMEM((2, nz, LANES), f32),
                pltpu.VMEM((2, nz, LANES), f32),
                pltpu.VMEM((2, 3, nx, ny), f32),
                pltpu.VMEM((2, 3, nx, ny), f32),
                pltpu.VMEM((group, 2, nx, ny), jnp.int32),
                pltpu.VMEM((group, 3, nx, ny), f32),
                pltpu.VMEM((3 * PARTS * fx, columns), jnp.bfloat16),
                pltpu.VMEM((fy, columns), jnp.bfloat16),
                pltpu.VMEM((6, fx + 16, fy), f32),
                pltpu.VMEM((fx, fy), jnp.int32),
                pltpu.VMEM((3, fx, fy), f32),
                pltpu.VMEM((2, 8, fy), f32),
                pltpu.VMEM((2, 8, fy), f32),
                pltpu.VMEM((2, fx, LANES), f32),
                pltpu.VMEM((2, fx, LANES), f32),
                pltpu.VMEM((3, fx, fy), f32),
                pltpu.SemaphoreType.DMA((6,)),
                pltpu.SemaphoreType.DMA((10,)),
                pltpu.SemaphoreType.DMA((10,)),
                pltpu.SemaphoreType.DMA((group,)),
                pltpu.SemaphoreType.DMA((group,)),
                pltpu.SemaphoreType.DMA((group,)),
                pltpu.SemaphoreType.DMA((group,)),
            ],
            compiler_params=pltpu.CompilerParams(
                collective_id=0, has_side_effects=True, vmem_limit_bytes=48 * 1024 * 1024),
        )(near_state, ids, far, wet_mask)

    return jax.shard_map(
        local,
        mesh=mesh,
        in_specs=(
            P(None, "px", "dz", "py"),
            P("px", ("py", "dz"), None, None),
            P("px", ("py", "dz"), None),
            P("px", ("py", "dz")),
            P(None, "px", ("py", "dz")),
            P("px", ("py", "dz")),
        ),
        out_specs=(P("px", "dz", "py"), P(None, "px", ("py", "dz"))),
        check_vma=False,
    )
```

```python
import functools

import jax
import jax.numpy as jnp
from jax import lax
from jax.experimental import pallas as pl
from jax.experimental.pallas import tpu as pltpu
from jax.sharding import PartitionSpec as P

advect_coef = 0.25
diffuse_coef = 0.1
slope_coef = 0.5
flux_coef = 0.1
gravity = 1.0
column_height = 4.0

LANES = 128
PARTS = 2


def kernel(sizes, near, own_in, land_in, dep_in, flow_in, wet_in, frac_out, far_out,
           x, nf, fout, idraw, yedge, yhalo, zedge, zhalo, idall, sums, a_mat, b_mat, q, wet, fdep, fedge_r, fhalo_r, fedge_c, fhalo_c,
           loc_sem, hs, hr, ids_s, ids_r, sum_s, sum_r):
    n_px, n_py, n_dz = sizes
    group = n_py * n_dz
    nx, nz, ny = near.shape[1:]
    fx, fy = wet_in.shape
    px, py, dz = lax.axis_index("px"), lax.axis_index("py"), lax.axis_index("dz")
    me = py * n_dz + dz

    def member(d):
        return {"px": px, "py": d // n_dz, "dz": d % n_dz}

    def peer(o):
        return lax.rem(me + o, group)

    def source(o):
        return lax.rem(me + group - o, group)

    up, down = {"px": px + 1, "py": py, "dz": dz}, {"px": px - 1, "py": py, "dz": dz}
    has_up, has_down = px < n_px - 1, px > 0

    barrier = pltpu.get_barrier_semaphore()
    for o in range(1, group):
        pl.semaphore_signal(barrier, inc=1, device_id=member(peer(o)))

    @pl.when(has_up)
    def _():
        pl.semaphore_signal(barrier, inc=1, device_id=up)

    @pl.when(has_down)
    def _():
        pl.semaphore_signal(barrier, inc=1, device_id=down)

    load_x = pltpu.make_async_copy(near, x.at[:, pl.ds(1, nx), pl.ds(8, nz), :], loc_sem.at[0])
    load_dep = pltpu.make_async_copy(dep_in, fdep.at[0], loc_sem.at[1])
    load_flow = pltpu.make_async_copy(flow_in, fdep.at[pl.ds(1, 2)], loc_sem.at[4])
    load_wet = pltpu.make_async_copy(wet_in, wet, loc_sem.at[2])
    load_own = pltpu.make_async_copy(own_in.at[0], idraw.at[0], loc_sem.at[3])
    load_land = pltpu.make_async_copy(land_in.at[0], idraw.at[1], loc_sem.at[5])
    loads = (load_x, load_own, load_land, load_dep, load_flow, load_wet)
    for load in loads:
        load.start()

    pl.semaphore_wait(barrier, group - 1 + has_up.astype(jnp.int32) + has_down.astype(jnp.int32))

    def send(src, dst, i, where):
        return pltpu.make_async_remote_copy(src_ref=src, dst_ref=dst, send_sem=hs.at[i], recv_sem=hr.at[i], device_id=where)

    rows = pl.ds(8, nz)
    x_up = send(near.at[:, nx - 1], x.at[:, 0, rows, :], 0, up)
    x_down = send(near.at[:, 0], x.at[:, nx + 1, rows, :], 1, down)
    y_up = send(yedge.at[0], yhalo.at[0], 2, {"px": px, "py": py + 1, "dz": dz})
    y_down = send(yedge.at[1], yhalo.at[1], 3, {"px": px, "py": py - 1, "dz": dz})
    z_up = send(zedge.at[0], zhalo.at[0], 4, {"px": px, "py": py, "dz": dz + 1})
    z_down = send(zedge.at[1], zhalo.at[1], 5, {"px": px, "py": py, "dz": dz - 1})
    fr_up = send(fedge_r.at[0], fhalo_r.at[0], 6, up)
    fr_down = send(fedge_r.at[1], fhalo_r.at[1], 7, down)
    fc_up = send(fedge_c.at[0], fhalo_c.at[0], 8, member(me + 1))
    fc_down = send(fedge_c.at[1], fhalo_c.at[1], 9, member(me - 1))
    near_y = ((y_up, py < n_py - 1, py > 0, yhalo.at[0]), (y_down, py > 0, py < n_py - 1, yhalo.at[1]))
    near_z = ((z_up, dz < n_dz - 1, dz > 0, zhalo.at[0]), (z_down, dz > 0, dz < n_dz - 1, zhalo.at[1]))
    near_x = ((x_up, has_up, has_down, x.at[:, 0]), (x_down, has_down, has_up, x.at[:, nx + 1]))
    far_r = ((fr_up, has_up, has_down, fhalo_r.at[0]), (fr_down, has_down, has_up, fhalo_r.at[1]))
    far_c = ((fc_up, me < group - 1, me > 0, fhalo_c.at[0]), (fc_down, me > 0, me < group - 1, fhalo_c.at[1]))

    def start(pairs):
        for copy, out, _, _ in pairs:
            pl.when(out)(copy.start)

    def clear(pairs):
        for _, _, into, halo in pairs:
            @pl.when(jnp.logical_not(into))
            def _():
                halo[...] = jnp.zeros(halo.shape, jnp.float32)

    def arrive(pairs):
        for copy, _, into, _ in pairs:
            pl.when(into)(copy.wait_recv)

    def sent(pairs):
        for copy, out, _, _ in pairs:
            pl.when(out)(copy.wait_send)

    start(near_x)
    for pairs in (near_x, near_y, near_z, far_r, far_c):
        clear(pairs)

    load_x.wait()
    lane = lax.broadcasted_iota(jnp.int32, (nz, LANES), 1)
    for f in range(3):
        for i in range(nx):
            zedge[0, f, pl.ds(i, 1), :] = x[f, i + 1, pl.ds(nz + 7, 1), :]
            zedge[1, f, pl.ds(i, 1), :] = x[f, i + 1, pl.ds(8, 1), :]
    start(near_z)
    high = jnp.zeros((nz, LANES), jnp.float32)
    low = jnp.zeros((nz, LANES), jnp.float32)
    for i in range(nx):
        for f in range(3):
            k = 3 * i + f
            high = jnp.where(lane == k, pltpu.roll(x[f, i + 1, rows, ny - LANES:], (k + 1) % LANES, 1), high)
            first = x[f, i + 1, rows, :LANES]
            low = jnp.where(lane == k, pltpu.roll(first, k, 1) if k else first, low)
    yedge[0] = high
    yedge[1] = low
    start(near_y)

    load_own.wait()
    load_land.wait()
    count = idraw.shape[2]
    qy = count // nx
    level = lax.broadcasted_iota(jnp.int32, (nx, ny), 0)
    along = lax.broadcasted_iota(jnp.int32, (nx, ny), 1)
    mine = jnp.logical_and(along >= dz * qy, along < (dz + 1) * qy)
    for t in range(2):
        raw = jnp.broadcast_to(idraw[t], (nx, count))
        placed = jnp.zeros((nx, ny), jnp.int32)
        for i in range(nx):
            turned = pltpu.roll(raw, lax.rem(dz * qy + (count - i * qy), count), 1)[:, :ny]
            placed = jnp.where(jnp.logical_and(level == i, mine), turned, placed)
        idall[me, t] = placed

    def id_copy(o, d):
        return pltpu.make_async_remote_copy(
            src_ref=idall.at[me], dst_ref=idall.at[d], send_sem=ids_s.at[o], recv_sem=ids_r.at[o], device_id=member(peer(o)))

    for o in range(1, group):
        id_copy(o, me).start()

    arrive(near_z)
    for f in range(3):
        for i in range(nx):
            x[f, i + 1, pl.ds(7, 1), :] = zhalo[0, f, pl.ds(i, 1), :]
            x[f, i + 1, pl.ds(nz + 8, 1), :] = zhalo[1, f, pl.ds(i, 1), :]
    arrive(near_y)

    col = lax.broadcasted_iota(jnp.int32, (8, ny), 1)

    def plane(i):
        total = [jnp.zeros((8, ny), jnp.float32) for _ in range(3)]
        shift = (LANES - 3 * i) % LANES if isinstance(i, int) else lax.rem(LANES - 3 * i, LANES)
        for c in range(0, nz, 8):
            here = pl.ds(8 + c, 8)
            ylo = pltpu.roll(yhalo[0, pl.ds(c, 8), :], shift, 1)
            yhi = pltpu.roll(yhalo[1, pl.ds(c, 8), :], shift, 1)
            u, v = x[1, i + 1, here, :], x[2, i + 1, here, :]
            moved, slopes = [], None
            for f in range(3):
                mid = x[f, i + 1, here, :]
                xp, xm = x[f, i + 2, here, :], x[f, i, here, :]
                zp, zm = x[f, i + 1, pl.ds(9 + c, 8), :], x[f, i + 1, pl.ds(7 + c, 8), :]
                yp = jnp.where(col == ny - 1, yhi[:, f:f + 1], pltpu.roll(mid, ny - 1, 1))
                ym = jnp.where(col == 0, ylo[:, f:f + 1], pltpu.roll(mid, 1, 1))
                dx, dy = xp - xm, yp - ym
                lap = xp + xm + yp + ym + zp + zm - 6.0 * mid
                moved.append(mid - advect_coef * (u * dx + v * dy) + diffuse_coef * lap)
                if f == 0:
                    slopes = (dx, dy)
            nf[i, pl.ds(c, 8), :] = moved[0]
            total[0] += moved[0]
            total[1] += moved[0] * (moved[1] - slope_coef * slopes[0])
            total[2] += moved[0] * (moved[2] - slope_coef * slopes[1])
        for f in range(3):
            sums[me, f, pl.ds(i, 1), :] = jnp.sum(total[f], axis=0, keepdims=True)

    def inner(i, carry):
        plane(i)
        return carry

    lax.fori_loop(1, nx - 1, inner, 0)

    for o in range(1, group):
        id_copy(o, source(o)).wait_recv()
    row_at = []
    line = lax.broadcasted_iota(jnp.int32, (fy, ny), 0)
    for p in range(n_py):
        owner, land = idall[p * n_dz, 0], idall[p * n_dz, 1]
        for e in range(1, n_dz):
            owner = owner + idall[p * n_dz + e, 0]
            land = land + idall[p * n_dz + e, 1]
        row = lax.div(land, jnp.full_like(land, fy)) if fy & (fy - 1) else lax.shift_right_logical(land, jnp.full_like(land, fy.bit_length() - 1))
        at = land - row * fy
        row_at.append(jnp.where(owner == me, row, -1))
        for i in range(nx):
            b = (p * nx + i) * ny
            b_mat[:, pl.ds(b, ny)] = jnp.where(line == at[i:i + 1, :], 1.0, 0.0).astype(jnp.bfloat16)

    arrive(near_x)
    plane(0)
    plane(nx - 1)

    def sum_copy(o, d):
        return pltpu.make_async_remote_copy(
            src_ref=sums.at[me], dst_ref=sums.at[d], send_sem=sum_s.at[o], recv_sem=sum_r.at[o], device_id=member(peer(o)))

    for o in range(1, group):
        sum_copy(o, me).start()
    save_frac = pltpu.make_async_copy(nf, frac_out, loc_sem.at[6])
    save_frac.start()
    load_dep.wait()
    load_flow.wait()
    load_wet.wait()
    for o in range(1, group):
        sum_copy(o, source(o)).wait_recv()

    per_column = column_height / (nz * n_dz)
    cell_row = lax.broadcasted_iota(jnp.int32, (fx, ny), 0)
    for p in range(n_py):
        parts = []
        for f in range(3):
            rest = sums[p * n_dz, f]
            for e in range(1, n_dz):
                rest = rest + sums[p * n_dz + e, f]
            rest = rest * per_column
            for s in range(PARTS):
                part = rest.astype(jnp.bfloat16).astype(jnp.float32)
                rest = rest - part
                parts.append(part)
        for i in range(nx):
            b = (p * nx + i) * ny
            hit = cell_row == row_at[p][i:i + 1, :]
            for k, part in enumerate(parts):
                a_mat[pl.ds(k * fx, fx), pl.ds(b, ny)] = jnp.where(hit, part[i:i + 1, :], 0.0).astype(jnp.bfloat16)
    landed = lax.dot_general(a_mat[...], b_mat[...], (((1,), (1,)), ((), ())), preferred_element_type=jnp.float32)
    dry = wet[...].astype(jnp.float32)
    for f in range(3):
        state = fdep[f]
        for s in range(PARTS):
            k = f * PARTS + s
            state = state + landed[k * fx:(k + 1) * fx, :]
        if f:
            state = state * dry
        q[f, pl.ds(8, fx), :] = state
        fedge_r[0, pl.ds(f, 1), :] = state[fx - 1:fx, :]
        fedge_r[1, pl.ds(f, 1), :] = state[0:1, :]
    start(far_r)
    lane = lax.broadcasted_iota(jnp.int32, (fx, LANES), 1)
    high = jnp.zeros((fx, LANES), jnp.float32)
    low = jnp.zeros((fx, LANES), jnp.float32)
    for f in range(3):
        high = jnp.where(lane == f, pltpu.roll(q[f, pl.ds(8, fx), fy - LANES:], f + 1, 1), high)
        first = q[f, pl.ds(8, fx), :LANES]
        low = jnp.where(lane == f, pltpu.roll(first, f, 1) if f else first, low)
    fedge_c[0] = high
    fedge_c[1] = low
    start(far_c)

    def fluxes(h, hu, hv, divisor):
        inverse = 1.0 / divisor
        press = 0.5 * gravity * h * h
        return hu * hu * inverse + press, hu * hv * inverse, hv * hv * inverse + press

    for c in range(8, fx + 8, 8):
        here = pl.ds(c, 8)
        h, hu, hv = q[0, here, :], q[1, here, :], q[2, here, :]
        for k, flux in enumerate(fluxes(h, hu, hv, h)):
            q[3 + k, here, :] = flux

    arrive(far_r)
    for side, there, at in ((0, has_down, 7), (1, has_up, fx + 8)):
        h, hu, hv = (fhalo_r[side, pl.ds(f, 1), :] for f in range(3))
        for k, value in enumerate((h, hu, hv) + fluxes(h, hu, hv, jnp.where(there, h, 1.0))):
            q[k, pl.ds(at, 1), :] = value
    arrive(far_c)
    col = lax.broadcasted_iota(jnp.int32, (8, fy), 1)
    for c in range(0, fx, 8):
        here = pl.ds(8 + c, 8)
        outer = []
        for side, there in ((0, me > 0), (1, me < group - 1)):
            block = fhalo_c[side, pl.ds(c, 8), :]
            h, hu, hv = block, pltpu.roll(block, LANES - 1, 1), pltpu.roll(block, LANES - 2, 1)
            outer.append([z[:, 0:1] for z in (h, hu, hv) + fluxes(h, hu, hv, jnp.where(there, h, 1.0))])

        def beside(k):
            mid = q[k, here, :]
            return (jnp.where(col == fy - 1, outer[1][k], pltpu.roll(mid, fy - 1, 1)),
                    jnp.where(col == 0, outer[0][k], pltpu.roll(mid, 1, 1)))

        above = [q[k, pl.ds(9 + c, 8), :] for k in range(5)]
        below = [q[k, pl.ds(7 + c, 8), :] for k in range(5)]
        pairs = [beside(0), beside(1), beside(2), None, beside(4), beside(5)]
        for f, (xk, yk) in enumerate(((1, 2), (3, 4), (4, 5))):
            mean = 0.25 * (above[f] + below[f] + pairs[f][0] + pairs[f][1])
            fout[f, pl.ds(c, 8), :] = (
                mean - flux_coef * (above[xk] - below[xk]) - flux_coef * (pairs[yk][0] - pairs[yk][1]))

    save_far = pltpu.make_async_copy(fout, far_out, loc_sem.at[7])
    save_far.start()
    for pairs in (near_x, near_y, near_z, far_r, far_c):
        sent(pairs)
    for o in range(1, group):
        id_copy(o, me).wait_send()
        sum_copy(o, me).wait_send()
    save_frac.wait()
    save_far.wait()


def solution(mesh):
    sizes = tuple(mesh.shape[axis] for axis in ("px", "py", "dz"))
    n_px, n_py, n_dz = sizes
    group = n_py * n_dz

    def local(near_state, column_owner, landing, far_depth, far_flows, wet_mask):
        nx, nz, ny = near_state.shape[1:]
        fx, fy = far_depth.shape
        kept = pl.BlockSpec(memory_space=pltpu.HBM)
        f32 = jnp.float32
        columns = n_py * nx * ny
        return pl.pallas_call(
            functools.partial(kernel, sizes),
            out_shape=(jax.ShapeDtypeStruct((nx, nz, ny), f32), jax.ShapeDtypeStruct((3, fx, fy), f32)),
            in_specs=[kept] * 6,
            out_specs=(kept, kept),
            scratch_shapes=[
                pltpu.VMEM((3, nx + 2, nz + 16, ny), f32),
                pltpu.VMEM((nx, nz, ny), f32),
                pltpu.VMEM((3, fx, fy), f32),
                pltpu.VMEM((2, 1, landing.shape[2]), jnp.int32),
                pltpu.VMEM((2, nz, LANES), f32),
                pltpu.VMEM((2, nz, LANES), f32),
                pltpu.VMEM((2, 3, nx, ny), f32),
                pltpu.VMEM((2, 3, nx, ny), f32),
                pltpu.VMEM((group, 2, nx, ny), jnp.int32),
                pltpu.VMEM((group, 3, nx, ny), f32),
                pltpu.VMEM((3 * PARTS * fx, columns), jnp.bfloat16),
                pltpu.VMEM((fy, columns), jnp.bfloat16),
                pltpu.VMEM((6, fx + 16, fy), f32),
                pltpu.VMEM((fx, fy), jnp.int32),
                pltpu.VMEM((3, fx, fy), f32),
                pltpu.VMEM((2, 8, fy), f32),
                pltpu.VMEM((2, 8, fy), f32),
                pltpu.VMEM((2, fx, LANES), f32),
                pltpu.VMEM((2, fx, LANES), f32),
                pltpu.SemaphoreType.DMA((8,)),
                pltpu.SemaphoreType.DMA((10,)),
                pltpu.SemaphoreType.DMA((10,)),
                pltpu.SemaphoreType.DMA((group,)),
                pltpu.SemaphoreType.DMA((group,)),
                pltpu.SemaphoreType.DMA((group,)),
                pltpu.SemaphoreType.DMA((group,)),
            ],
            compiler_params=pltpu.CompilerParams(
                collective_id=0, has_side_effects=True, vmem_limit_bytes=63 * 1024 * 1024),
        )(near_state, column_owner.reshape(landing.shape), landing, far_depth, far_flows, wet_mask)

    return jax.shard_map(
        local,
        mesh=mesh,
        in_specs=(
            P(None, "px", "dz", "py"),
            P("px", ("py", "dz"), None, None),
            P("px", ("py", "dz"), None),
            P("px", ("py", "dz")),
            P(None, "px", ("py", "dz")),
            P("px", ("py", "dz")),
        ),
        out_specs=(P("px", "dz", "py"), P(None, "px", ("py", "dz"))),
        check_vma=False,
    )
```

```python
import functools

import jax
import jax.numpy as jnp
from jax import lax
from jax.experimental import pallas as pl
from jax.experimental.pallas import tpu as pltpu
from jax.sharding import PartitionSpec as P

advect_coef = 0.25
diffuse_coef = 0.1
slope_coef = 0.5
flux_coef = 0.1
gravity = 1.0
column_height = 4.0

LANES = 128
PARTS = 2


def kernel(sizes, near, own_in, land_in, dep_in, flow_in, wet_in, nf, fout,
           x, idraw, yedge, yhalo, zedge, zhalo, idall, sums, a_mat, b_mat, q, wet, fdep, fedge_r, fhalo_r, fedge_c, fhalo_c,
           loc_sem, hs, hr, ids_s, ids_r, sum_s, sum_r):
    n_px, n_py, n_dz = sizes
    group = n_py * n_dz
    nx, nz, ny = near.shape[1:]
    fx, fy = wet_in.shape
    px, py, dz = lax.axis_index("px"), lax.axis_index("py"), lax.axis_index("dz")
    me = py * n_dz + dz

    def member(d):
        return {"px": px, "py": d // n_dz, "dz": d % n_dz}

    def peer(o):
        return lax.rem(me + o, group)

    def source(o):
        return lax.rem(me + group - o, group)

    up, down = {"px": px + 1, "py": py, "dz": dz}, {"px": px - 1, "py": py, "dz": dz}
    has_up, has_down = px < n_px - 1, px > 0

    barrier = pltpu.get_barrier_semaphore()
    for o in range(1, group):
        pl.semaphore_signal(barrier, inc=1, device_id=member(peer(o)))

    @pl.when(has_up)
    def _():
        pl.semaphore_signal(barrier, inc=1, device_id=up)

    @pl.when(has_down)
    def _():
        pl.semaphore_signal(barrier, inc=1, device_id=down)

    load_x = pltpu.make_async_copy(near, x.at[:, pl.ds(1, nx), pl.ds(8, nz), :], loc_sem.at[0])
    load_dep = pltpu.make_async_copy(dep_in, fdep.at[0], loc_sem.at[1])
    load_flow = pltpu.make_async_copy(flow_in, fdep.at[pl.ds(1, 2)], loc_sem.at[4])
    load_wet = pltpu.make_async_copy(wet_in, wet, loc_sem.at[2])
    load_own = pltpu.make_async_copy(own_in.at[0], idraw.at[0], loc_sem.at[3])
    load_land = pltpu.make_async_copy(land_in.at[0], idraw.at[1], loc_sem.at[5])
    loads = (load_x, load_own, load_land, load_dep, load_flow, load_wet)
    for load in loads:
        load.start()

    pl.semaphore_wait(barrier, group - 1 + has_up.astype(jnp.int32) + has_down.astype(jnp.int32))

    def send(src, dst, i, where):
        return pltpu.make_async_remote_copy(src_ref=src, dst_ref=dst, send_sem=hs.at[i], recv_sem=hr.at[i], device_id=where)

    rows = pl.ds(8, nz)
    x_up = send(near.at[:, nx - 1], x.at[:, 0, rows, :], 0, up)
    x_down = send(near.at[:, 0], x.at[:, nx + 1, rows, :], 1, down)
    y_up = send(yedge.at[0], yhalo.at[0], 2, {"px": px, "py": py + 1, "dz": dz})
    y_down = send(yedge.at[1], yhalo.at[1], 3, {"px": px, "py": py - 1, "dz": dz})
    z_up = send(zedge.at[0], zhalo.at[0], 4, {"px": px, "py": py, "dz": dz + 1})
    z_down = send(zedge.at[1], zhalo.at[1], 5, {"px": px, "py": py, "dz": dz - 1})
    fr_up = send(fedge_r.at[0], fhalo_r.at[0], 6, up)
    fr_down = send(fedge_r.at[1], fhalo_r.at[1], 7, down)
    fc_up = send(fedge_c.at[0], fhalo_c.at[0], 8, member(me + 1))
    fc_down = send(fedge_c.at[1], fhalo_c.at[1], 9, member(me - 1))
    near_y = ((y_up, py < n_py - 1, py > 0, yhalo.at[0]), (y_down, py > 0, py < n_py - 1, yhalo.at[1]))
    near_z = ((z_up, dz < n_dz - 1, dz > 0, zhalo.at[0]), (z_down, dz > 0, dz < n_dz - 1, zhalo.at[1]))
    near_x = ((x_up, has_up, has_down, x.at[:, 0]), (x_down, has_down, has_up, x.at[:, nx + 1]))
    far_r = ((fr_up, has_up, has_down, fhalo_r.at[0]), (fr_down, has_down, has_up, fhalo_r.at[1]))
    far_c = ((fc_up, me < group - 1, me > 0, fhalo_c.at[0]), (fc_down, me > 0, me < group - 1, fhalo_c.at[1]))

    def start(pairs):
        for copy, out, _, _ in pairs:
            pl.when(out)(copy.start)

    def clear(pairs):
        for _, _, into, halo in pairs:
            @pl.when(jnp.logical_not(into))
            def _():
                halo[...] = jnp.zeros(halo.shape, jnp.float32)

    def arrive(pairs):
        for copy, _, into, _ in pairs:
            pl.when(into)(copy.wait_recv)

    def sent(pairs):
        for copy, out, _, _ in pairs:
            pl.when(out)(copy.wait_send)

    start(near_x)
    for pairs in (near_x, near_y, near_z, far_r, far_c):
        clear(pairs)

    load_x.wait()
    lane = lax.broadcasted_iota(jnp.int32, (nz, LANES), 1)
    for f in range(3):
        for i in range(nx):
            zedge[0, f, pl.ds(i, 1), :] = x[f, i + 1, pl.ds(nz + 7, 1), :]
            zedge[1, f, pl.ds(i, 1), :] = x[f, i + 1, pl.ds(8, 1), :]
    start(near_z)
    high = jnp.zeros((nz, LANES), jnp.float32)
    low = jnp.zeros((nz, LANES), jnp.float32)
    for i in range(nx):
        for f in range(3):
            k = 3 * i + f
            high = jnp.where(lane == k, pltpu.roll(x[f, i + 1, rows, ny - LANES:], (k + 1) % LANES, 1), high)
            first = x[f, i + 1, rows, :LANES]
            low = jnp.where(lane == k, pltpu.roll(first, k, 1) if k else first, low)
    yedge[0] = high
    yedge[1] = low
    start(near_y)

    load_own.wait()
    load_land.wait()
    count = idraw.shape[2]
    qy = count // nx
    level = lax.broadcasted_iota(jnp.int32, (nx, ny), 0)
    along = lax.broadcasted_iota(jnp.int32, (nx, ny), 1)
    mine = jnp.logical_and(along >= dz * qy, along < (dz + 1) * qy)
    for t in range(2):
        raw = jnp.broadcast_to(idraw[t], (nx, count))
        placed = jnp.zeros((nx, ny), jnp.int32)
        for i in range(nx):
            turned = pltpu.roll(raw, lax.rem(dz * qy + (count - i * qy), count), 1)[:, :ny]
            placed = jnp.where(jnp.logical_and(level == i, mine), turned, placed)
        idall[me, t] = placed

    def id_copy(o, d):
        return pltpu.make_async_remote_copy(
            src_ref=idall.at[me], dst_ref=idall.at[d], send_sem=ids_s.at[o], recv_sem=ids_r.at[o], device_id=member(peer(o)))

    for o in range(1, group):
        id_copy(o, me).start()

    arrive(near_z)
    for f in range(3):
        for i in range(nx):
            x[f, i + 1, pl.ds(7, 1), :] = zhalo[0, f, pl.ds(i, 1), :]
            x[f, i + 1, pl.ds(nz + 8, 1), :] = zhalo[1, f, pl.ds(i, 1), :]
    arrive(near_y)

    col = lax.broadcasted_iota(jnp.int32, (8, ny), 1)

    def plane(i):
        total = [jnp.zeros((8, ny), jnp.float32) for _ in range(3)]
        shift = (LANES - 3 * i) % LANES if isinstance(i, int) else lax.rem(LANES - 3 * i, LANES)
        for c in range(0, nz, 8):
            here = pl.ds(8 + c, 8)
            ylo = pltpu.roll(yhalo[0, pl.ds(c, 8), :], shift, 1)
            yhi = pltpu.roll(yhalo[1, pl.ds(c, 8), :], shift, 1)
            u, v = x[1, i + 1, here, :], x[2, i + 1, here, :]
            moved, slopes = [], None
            for f in range(3):
                mid = x[f, i + 1, here, :]
                xp, xm = x[f, i + 2, here, :], x[f, i, here, :]
                zp, zm = x[f, i + 1, pl.ds(9 + c, 8), :], x[f, i + 1, pl.ds(7 + c, 8), :]
                yp = jnp.where(col == ny - 1, yhi[:, f:f + 1], pltpu.roll(mid, ny - 1, 1))
                ym = jnp.where(col == 0, ylo[:, f:f + 1], pltpu.roll(mid, 1, 1))
                dx, dy = xp - xm, yp - ym
                lap = xp + xm + yp + ym + zp + zm - 6.0 * mid
                moved.append(mid - advect_coef * (u * dx + v * dy) + diffuse_coef * lap)
                if f == 0:
                    slopes = (dx, dy)
            nf[i, pl.ds(c, 8), :] = moved[0]
            total[0] += moved[0]
            total[1] += moved[0] * (moved[1] - slope_coef * slopes[0])
            total[2] += moved[0] * (moved[2] - slope_coef * slopes[1])
        for f in range(3):
            sums[me, f, pl.ds(i, 1), :] = jnp.sum(total[f], axis=0, keepdims=True)

    def inner(i, carry):
        plane(i)
        return carry

    lax.fori_loop(1, nx - 1, inner, 0)

    for o in range(1, group):
        id_copy(o, source(o)).wait_recv()
    row_at = []
    line = lax.broadcasted_iota(jnp.int32, (fy, ny), 0)
    for p in range(n_py):
        owner, land = idall[p * n_dz, 0], idall[p * n_dz, 1]
        for e in range(1, n_dz):
            owner = owner + idall[p * n_dz + e, 0]
            land = land + idall[p * n_dz + e, 1]
        row = lax.div(land, jnp.full_like(land, fy)) if fy & (fy - 1) else lax.shift_right_logical(land, jnp.full_like(land, fy.bit_length() - 1))
        at = land - row * fy
        row_at.append(jnp.where(owner == me, row, -1))
        for i in range(nx):
            b = (p * nx + i) * ny
            b_mat[:, pl.ds(b, ny)] = jnp.where(line == at[i:i + 1, :], 1.0, 0.0).astype(jnp.bfloat16)

    arrive(near_x)
    plane(0)
    plane(nx - 1)

    def sum_copy(o, d):
        return pltpu.make_async_remote_copy(
            src_ref=sums.at[me], dst_ref=sums.at[d], send_sem=sum_s.at[o], recv_sem=sum_r.at[o], device_id=member(peer(o)))

    for o in range(1, group):
        sum_copy(o, me).start()
    load_dep.wait()
    load_flow.wait()
    load_wet.wait()
    for o in range(1, group):
        sum_copy(o, source(o)).wait_recv()

    per_column = column_height / (nz * n_dz)
    cell_row = lax.broadcasted_iota(jnp.int32, (fx, ny), 0)
    for p in range(n_py):
        parts = []
        for f in range(3):
            rest = sums[p * n_dz, f]
            for e in range(1, n_dz):
                rest = rest + sums[p * n_dz + e, f]
            rest = rest * per_column
            for s in range(PARTS):
                part = rest.astype(jnp.bfloat16).astype(jnp.float32)
                rest = rest - part
                parts.append(part)
        for i in range(nx):
            b = (p * nx + i) * ny
            hit = cell_row == row_at[p][i:i + 1, :]
            for k, part in enumerate(parts):
                a_mat[pl.ds(k * fx, fx), pl.ds(b, ny)] = jnp.where(hit, part[i:i + 1, :], 0.0).astype(jnp.bfloat16)
    landed = lax.dot_general(a_mat[...], b_mat[...], (((1,), (1,)), ((), ())), preferred_element_type=jnp.float32)
    dry = wet[...].astype(jnp.float32)
    for f in range(3):
        state = fdep[f]
        for s in range(PARTS):
            k = f * PARTS + s
            state = state + landed[k * fx:(k + 1) * fx, :]
        if f:
            state = state * dry
        q[f, pl.ds(8, fx), :] = state
        fedge_r[0, pl.ds(f, 1), :] = state[fx - 1:fx, :]
        fedge_r[1, pl.ds(f, 1), :] = state[0:1, :]
    start(far_r)
    lane = lax.broadcasted_iota(jnp.int32, (fx, LANES), 1)
    high = jnp.zeros((fx, LANES), jnp.float32)
    low = jnp.zeros((fx, LANES), jnp.float32)
    for f in range(3):
        high = jnp.where(lane == f, pltpu.roll(q[f, pl.ds(8, fx), fy - LANES:], f + 1, 1), high)
        first = q[f, pl.ds(8, fx), :LANES]
        low = jnp.where(lane == f, pltpu.roll(first, f, 1) if f else first, low)
    fedge_c[0] = high
    fedge_c[1] = low
    start(far_c)

    def fluxes(h, hu, hv, divisor):
        inverse = 1.0 / divisor
        press = 0.5 * gravity * h * h
        return hu * hu * inverse + press, hu * hv * inverse, hv * hv * inverse + press

    for c in range(8, fx + 8, 8):
        here = pl.ds(c, 8)
        h, hu, hv = q[0, here, :], q[1, here, :], q[2, here, :]
        for k, flux in enumerate(fluxes(h, hu, hv, h)):
            q[3 + k, here, :] = flux

    arrive(far_r)
    for side, there, at in ((0, has_down, 7), (1, has_up, fx + 8)):
        h, hu, hv = (fhalo_r[side, pl.ds(f, 1), :] for f in range(3))
        for k, value in enumerate((h, hu, hv) + fluxes(h, hu, hv, jnp.where(there, h, 1.0))):
            q[k, pl.ds(at, 1), :] = value
    arrive(far_c)
    col = lax.broadcasted_iota(jnp.int32, (8, fy), 1)
    for c in range(0, fx, 8):
        here = pl.ds(8 + c, 8)
        outer = []
        for side, there in ((0, me > 0), (1, me < group - 1)):
            block = fhalo_c[side, pl.ds(c, 8), :]
            h, hu, hv = block, pltpu.roll(block, LANES - 1, 1), pltpu.roll(block, LANES - 2, 1)
            outer.append([z[:, 0:1] for z in (h, hu, hv) + fluxes(h, hu, hv, jnp.where(there, h, 1.0))])

        def beside(k):
            mid = q[k, here, :]
            return (jnp.where(col == fy - 1, outer[1][k], pltpu.roll(mid, fy - 1, 1)),
                    jnp.where(col == 0, outer[0][k], pltpu.roll(mid, 1, 1)))

        above = [q[k, pl.ds(9 + c, 8), :] for k in range(5)]
        below = [q[k, pl.ds(7 + c, 8), :] for k in range(5)]
        pairs = [beside(0), beside(1), beside(2), None, beside(4), beside(5)]
        for f, (xk, yk) in enumerate(((1, 2), (3, 4), (4, 5))):
            mean = 0.25 * (above[f] + below[f] + pairs[f][0] + pairs[f][1])
            fout[f, pl.ds(c, 8), :] = (
                mean - flux_coef * (above[xk] - below[xk]) - flux_coef * (pairs[yk][0] - pairs[yk][1]))

    for pairs in (near_x, near_y, near_z, far_r, far_c):
        sent(pairs)
    for o in range(1, group):
        id_copy(o, me).wait_send()
        sum_copy(o, me).wait_send()


def solution(mesh):
    sizes = tuple(mesh.shape[axis] for axis in ("px", "py", "dz"))
    n_px, n_py, n_dz = sizes
    group = n_py * n_dz

    def local(near_state, column_owner, landing, far_depth, far_flows, wet_mask):
        nx, nz, ny = near_state.shape[1:]
        fx, fy = far_depth.shape
        kept = pl.BlockSpec(memory_space=pltpu.HBM)
        f32 = jnp.float32
        columns = n_py * nx * ny
        return pl.pallas_call(
            functools.partial(kernel, sizes),
            out_shape=(pltpu.VMEM((nx, nz, ny), f32), pltpu.VMEM((3, fx, fy), f32)),
            in_specs=[kept] * 6,
            out_specs=(pl.BlockSpec(memory_space=pltpu.VMEM),) * 2,
            scratch_shapes=[
                pltpu.VMEM((3, nx + 2, nz + 16, ny), f32),
                pltpu.VMEM((2, 1, landing.shape[2]), jnp.int32),
                pltpu.VMEM((2, nz, LANES), f32),
                pltpu.VMEM((2, nz, LANES), f32),
                pltpu.VMEM((2, 3, nx, ny), f32),
                pltpu.VMEM((2, 3, nx, ny), f32),
                pltpu.VMEM((group, 2, nx, ny), jnp.int32),
                pltpu.VMEM((group, 3, nx, ny), f32),
                pltpu.VMEM((3 * PARTS * fx, columns), jnp.bfloat16),
                pltpu.VMEM((fy, columns), jnp.bfloat16),
                pltpu.VMEM((6, fx + 16, fy), f32),
                pltpu.VMEM((fx, fy), jnp.int32),
                pltpu.VMEM((3, fx, fy), f32),
                pltpu.VMEM((2, 8, fy), f32),
                pltpu.VMEM((2, 8, fy), f32),
                pltpu.VMEM((2, fx, LANES), f32),
                pltpu.VMEM((2, fx, LANES), f32),
                pltpu.SemaphoreType.DMA((8,)),
                pltpu.SemaphoreType.DMA((10,)),
                pltpu.SemaphoreType.DMA((10,)),
                pltpu.SemaphoreType.DMA((group,)),
                pltpu.SemaphoreType.DMA((group,)),
                pltpu.SemaphoreType.DMA((group,)),
                pltpu.SemaphoreType.DMA((group,)),
            ],
            compiler_params=pltpu.CompilerParams(
                collective_id=0, has_side_effects=True, vmem_limit_bytes=62 * 1024 * 1024),
        )(near_state, column_owner.reshape(landing.shape), landing, far_depth, far_flows, wet_mask)

    return jax.shard_map(
        local,
        mesh=mesh,
        in_specs=(
            P(None, "px", "dz", "py"),
            P("px", ("py", "dz"), None, None),
            P("px", ("py", "dz"), None),
            P("px", ("py", "dz")),
            P(None, "px", ("py", "dz")),
            P("px", ("py", "dz")),
        ),
        out_specs=(P("px", "dz", "py"), P(None, "px", ("py", "dz"))),
        check_vma=False,
    )
```
